1024 devices in a mesh: dp: 32 (over z), expert: 8 (over x, core), tensor: 4 (over y).
Axes of the slice: x: 4, y: 4, z: 32, core: 2. Of those that a mesh axis runs over, the one named last changes fastest.
Arguments:
- out_grad: bfloat16 [4096, 6144], P('expert', 'dp'), may hold values from -0.796875 to 0.796875
- expert_ids: int32 [4096, 2], P('expert'), may hold values from 0 to 7, all different within a row; in each aligned block of 512 rows (0 to 511, 512 to 1023, ...) at most 192 rows name the same one
- combine: float32 [4096, 2], P('expert'), may hold values from 0.2 to 1
- hidden: bfloat16 [8, 1536, 16384], P('expert', 'dp', 'tensor'), may hold values from -6 to 6
Outputs:
- grad_down: bfloat16 [8, 16384, 6144], P('expert', 'tensor', 'dp')
The draws below stay inside these ranges and needn't reach their ends.
Inputs may be any that keep to these rules, and one draw needn't show every extreme that they name: `expert_ids`: each row names 2 different experts; among the 512 rows of one device no expert is named more than 192 times.
All inputs are finite; a program needn't handle non-finite values.
Results may differ from the reference program's by a relative error of at most 0.0049.
Values may be sent and summed in bfloat16 or wider, within the bound.
No kernel may reach another device: no remote copies, remote signals or barrier semaphores. Data moves between devices by JAX's collectives and lax.ppermute only.
A program may use at most 64 MiB of HBM per device.

```python
import math
import jax
import jax.numpy as jnp
import numpy as np
from jax import lax

D = 6144
FF = 16384
TOP = 2
TOK_DEV = 512
EXPERTS = 8
TOKENS = 4096
MOST = 192
CAP = 1536


def steps_of(stream_key, extent, cuts, least, high):
    def one(position, parts):
        steps = jax.random.uniform(jax.random.fold_in(jax.random.fold_in(stream_key, 6), position), (parts,), jnp.float32, least / len(cuts), high / len(cuts))
        return jnp.repeat(jnp.exp(steps), extent[position] // parts).reshape((-1,) + (1,) * (len(extent) - position - 1))

    level = one(*cuts[0])
    for cut in cuts[1:]:
        level = level * one(*cut)
    return level


def routed_block(key, own, number, rows, amount, top, limit, slope):
    sequence = jax.random.permutation(key, amount)
    crowded, usual = shares(amount, rows * top, limit, slope, True), shares(amount, rows * top, limit, slope, False)
    places = jnp.arange(amount)

    def named(sizes, rotation):
        used = int((sizes > 0).sum())
        fixed = max(1, used // 4)
        passed = fixed + (places - fixed + rotation * (used - fixed)) % max(1, amount - fixed)
        return jnp.zeros((amount,), jnp.int32).at[sequence[jnp.where(places < fixed, places, passed)]].set(jnp.asarray(sizes, jnp.int32))

    sizes = jnp.where(number % 4 == 0, named(crowded, number // 4), named(usual, number - number // 4 - 1))
    mixed = jax.random.permutation(jax.random.fold_in(own, 3), amount)
    source_of, receiver = mixed[0:amount // 2 * 2:2], mixed[1:amount // 2 * 2:2]
    room = jnp.minimum(sizes[source_of] - 1, limit - sizes[receiver]) // 2
    room = jnp.where((source_of == sequence[0]) | (receiver == sequence[0]) | (sizes[receiver] == 0), 0, jnp.maximum(room, 0))
    passed = jax.random.randint(jax.random.fold_in(own, 4), (amount // 2,), 0, 1 << 20) % (room + 1)
    sizes = sizes.at[source_of].add(-passed).at[receiver].add(passed)
    labels = jnp.searchsorted(jnp.cumsum(sizes), jnp.arange(rows * top), side="right").astype(jnp.int32)
    listing = labels.reshape(top, rows).T
    listing = listing[jax.random.permutation(jax.random.fold_in(own, 1), rows)]
    rotation = jax.random.randint(jax.random.fold_in(own, 2), (rows, 1), 0, top)
    return jnp.take_along_axis(listing, (jnp.arange(top)[None, :] + rotation) % top, axis=1)


def shares(amount, total, bound, slope, full):
    portions = [(1 << 20) // math.isqrt(rank ** slope) + 1 for rank in range(1, amount + 1)]
    largest = bound if full else min(bound, max(-(-total // amount), total * portions[0] // sum(portions)))
    least = 1 if total - largest >= amount - 1 else 0
    holding, surplus = [largest] + [least] * (amount - 1), total - largest - least * (amount - 1)
    while surplus > 0:
        candidates = [i for i in range(1, amount) if holding[i] < largest] or [i for i in range(1, amount) if holding[i] < bound]
        whole, left = sum([portions[i] for i in candidates]), surplus
        for i in candidates:
            addition = min(bound - holding[i], max(1, left * portions[i] // whole), surplus)
            holding[i] = holding[i] + addition
            surplus = surplus - addition
    return np.array(holding)


def centred(stream_key, extent, deviation, bound, pieces=(), kind=jnp.bfloat16):
    drawn = jax.random.normal(stream_key, extent, jnp.float32) * deviation
    if len(pieces) > 0:
        drawn = steps_of(stream_key, extent, pieces, -0.22, 0.18) * drawn
    return jnp.clip(drawn, min=-bound, max=bound).astype(kind)


def setup_inputs(seed: int = 0) -> dict:
    seeds = jax.random.split(jax.random.key(seed), 5)
    out_grad = centred(seeds[0], (TOKENS, D), 0.1, 0.796875, ((0, 8), (1, 32)))
    expert_ids_keys = jax.random.split(jax.random.fold_in(seeds[1], 1), TOKENS // TOK_DEV)
    expert_ids_turns = jax.random.permutation(jax.random.fold_in(seeds[1], 3), TOKENS // TOK_DEV)
    expert_ids = jax.vmap(lambda own, number: routed_block(jax.random.fold_in(seeds[1], 2), own, number, TOK_DEV, EXPERTS, TOP, MOST, 2))(expert_ids_keys, expert_ids_turns).reshape((TOKENS, TOP))
    combine = jnp.clip(0.2 + 0.8 * jax.random.uniform(seeds[2], (TOKENS, TOP), jnp.float32) ** steps_of(seeds[2], (TOKENS, TOP), ((0, 8),), -0.2, 0.2), 0.2, 1.0)
    hidden = centred(seeds[3], (EXPERTS, CAP, FF), 1.0, 6.0, ((0, 8), (1, 32), (2, 4)))
    return {"out_grad": out_grad, "expert_ids": expert_ids, "combine": combine, "hidden": hidden}


def one_expert(pair):
    return lax.dot_general(pair[0], pair[1], (((0,), (0,)), ((), ())), preferred_element_type=jnp.float32).astype(jnp.bfloat16)


def reference(out_grad, expert_ids, combine, hidden):
    flat_ids = expert_ids.reshape(-1).astype(jnp.int32)
    onehot = (flat_ids[:, None] == jnp.arange(EXPERTS, dtype=jnp.int32)[None, :]).astype(jnp.int32)
    local_rank = jnp.sum((jnp.cumsum(onehot, axis=0) - onehot) * onehot, axis=1).astype(jnp.int32)
    scaled = (combine[:, :, None] * out_grad[:, None, :].astype(jnp.float32)).astype(jnp.bfloat16).reshape(-1, D)
    slot_index = flat_ids * CAP + local_rank
    arranged = jnp.zeros((EXPERTS * CAP, D), jnp.bfloat16).at[slot_index].set(scaled).reshape(EXPERTS, CAP, D)
    return lax.map(one_expert, (hidden, arranged))
```

```python
import jax
import jax.numpy as jnp
from jax import lax
from jax.experimental import pallas as pl
from jax.experimental.pallas import tpu as pltpu
from jax.sharding import PartitionSpec as P

LANES = 256
PAIRS = 16
COUNT = 192


def dot(a, b, da=1, db=0):
    return lax.dot_general(a, b, (((da,), (db,)), ((), ())), preferred_element_type=jnp.float32)


def send_kernel(ids_ref, weights_ref, first_ref, own_ref, second_ref, out_ref):
    features, tokens = own_ref.shape
    experts = out_ref.shape[0]
    ids, weights = ids_ref[...], weights_ref[...]
    lane = lax.broadcasted_iota(jnp.int32, (tokens, 128), 1)
    named = (ids[:, 0:1] == lane) | (ids[:, 1:2] == lane)
    earlier = lax.broadcasted_iota(jnp.int32, (tokens, tokens), 1) < lax.broadcasted_iota(
        jnp.int32, (tokens, tokens), 0
    )
    member = jnp.where(named, 1.0, 0.0).astype(jnp.bfloat16)
    ranks = dot(jnp.where(earlier, 1.0, 0.0).astype(jnp.bfloat16), member).astype(jnp.int32)
    ranks = jnp.where(named, ranks, -1)
    place = lax.broadcasted_iota(jnp.int32, (tokens, LANES), 1)
    for e in range(experts):
        chosen = place == ranks[:, e : e + 1]
        weight = jnp.where(ids[:, 0:1] == e, weights[:, 0:1], weights[:, 1:2])
        scale = jnp.sum(jnp.where(chosen, weight, 0.0), axis=0, keepdims=True)
        count = jnp.sum(jnp.where(ranks[:, e : e + 1] >= 0, 1.0, 0.0), axis=0, keepdims=True)
        pick = jnp.where(chosen, 1.0, 0.0).astype(jnp.bfloat16)
        at_count = lax.broadcasted_iota(jnp.int32, (features, LANES), 1) == COUNT
        for part, ref in enumerate((first_ref, own_ref, second_ref)):
            rows = dot(ref[...], pick) * scale
            out_ref[e, part * features : (part + 1) * features, :] = jnp.where(
                at_count, count, rows
            ).astype(jnp.bfloat16)


def place_kernel(base_ref, rows_ref, a_ref, b_ref, sums_a, sums_b):
    sources, wide, _ = rows_ref.shape
    height, capacity = a_ref.shape
    span = sums_a.shape[1] - capacity
    low = wide - height
    sums_a[...] = jnp.zeros_like(sums_a)
    sums_b[...] = jnp.zeros_like(sums_b)
    rank = lax.broadcasted_iota(jnp.int32, (LANES, 1), 0)
    lane = lax.broadcasted_iota(jnp.int32, (LANES, span), 1)
    spare = lax.broadcasted_iota(jnp.int32, (16, 128), 1) == COUNT - 128

    def source(i, offset):
        counts = rows_ref[i, 0:16, 128:256].astype(jnp.float32)
        count = jnp.max(jnp.where(spare, counts, 0.0)).astype(jnp.int32)
        for base, sums, rows in (
            (base_ref[0], sums_a, rows_ref[i, 0:height, :]),
            (base_ref[1], sums_b, rows_ref[i, low:, :]),
        ):
            slot = offset - base
            slot = jnp.where(slot < 0, slot + capacity, slot)
            start = pl.multiple_of((slot // 128) * 128, 128)
            goal = jnp.where(rank < count, rank + (slot - start), -1)
            pick = jnp.where(goal == lane, 1.0, 0.0).astype(jnp.bfloat16)
            sums[:, pl.ds(start, span)] += dot(rows, pick)
        return offset + count

    lax.fori_loop(0, sources, source, jnp.int32(0))
    for sums, out in ((sums_a, a_ref), (sums_b, b_ref)):
        out[:, 0:span] = (sums[:, 0:span] + sums[:, capacity:]).astype(jnp.bfloat16)
        out[:, span:] = sums[:, span:capacity].astype(jnp.bfloat16)


def near_kernel(*refs):
    arranged, blocks, out, held = refs[0], refs[1:-2], refs[-2], refs[-1]
    size = blocks[0].shape[0]
    for i, block in enumerate(blocks):
        held[i * size : (i + 1) * size, :] = block[...]
    out[...] = dot(arranged[...], held[...])


def far_kernel(*refs):
    total, arranged, blocks, (top, bottom), held = refs[0], refs[1], refs[2:-3], refs[-3:-1], refs[-1]
    size = blocks[0].shape[0]
    for i, block in enumerate(blocks):
        held[i * size : (i + 1) * size, :] = block[...]
    half = top.shape[0]
    top[...] = (total[0:half, :] + dot(arranged[0:half, :], held[...])).astype(jnp.bfloat16)
    bottom[...] = (total[half:, :] + dot(arranged[half:, :], held[...])).astype(jnp.bfloat16)


def params(megabytes):
    return pltpu.CompilerParams(vmem_limit_bytes=megabytes << 20)


def cost(flops, bytes_accessed):
    return pl.CostEstimate(flops=flops, bytes_accessed=bytes_accessed, transcendentals=0)


def scaled_rows(out_grad, expert_ids, combine, grad_a, grad_b, experts):
    features, tokens = out_grad.shape
    wide = 3 * features
    return pl.pallas_call(
        send_kernel,
        out_shape=jax.ShapeDtypeStruct((experts, wide, LANES), jnp.bfloat16),
        compiler_params=params(12),
        cost_estimate=cost(2 * experts * LANES * tokens * wide, 6 << 20),
    )(expert_ids, combine, grad_a, out_grad, grad_b)


def place(rows, even, z, share, near, features, capacity):
    experts, wide, _ = rows.shape
    base_a = share * (jnp.where(even, z, z - 1) - 2 * near)
    base_b = share * (jnp.where(even, z - 1, z) - 2 * near)
    bases = jnp.stack([base_a % capacity, base_b % capacity]).astype(jnp.int32)
    return pl.pallas_call(
        place_kernel,
        out_shape=[jax.ShapeDtypeStruct((2 * features, capacity), jnp.bfloat16)] * 2,
        in_specs=[
            pl.BlockSpec(memory_space=pltpu.SMEM),
            pl.BlockSpec(memory_space=pltpu.VMEM),
        ],
        scratch_shapes=[
            pltpu.VMEM((2 * features, capacity + 384), jnp.float32),
            pltpu.VMEM((2 * features, capacity + 384), jnp.float32),
        ],
        compiler_params=params(16),
        cost_estimate=cost(8 * features * experts * LANES * 384, 6 << 20),
    )(bases, rows)


def after(value, chain, s):
    return lax.optimization_barrier((value, chain[s], chain[PAIRS - s]))[0]


def before(values, chain, s):
    *values, chain[s], chain[PAIRS - s] = lax.optimization_barrier(
        (*values, chain[s], chain[PAIRS - s])
    )
    return values


def near_product(chain, arranged, near):
    depth = arranged.shape[1] // 2
    blocks = [chain[(d - near) % PAIRS] for d in range(2 * near)]
    quarter = blocks[0].shape[1]
    return pl.pallas_call(
        near_kernel,
        out_shape=jax.ShapeDtypeStruct((arranged.shape[0], quarter), jnp.float32),
        scratch_shapes=[pltpu.VMEM((depth, quarter), jnp.bfloat16)],
        compiler_params=params(12),
        cost_estimate=cost(2 * arranged.shape[0] * depth * quarter, 4 << 20),
    )(arranged[:, :depth], *blocks)


def far_product(total, chain, arranged, near):
    depth = arranged.shape[1] // 2
    blocks = [chain[(d - near) % PAIRS] for d in range(2 * near, PAIRS)]
    quarter = blocks[0].shape[1]
    half = jax.ShapeDtypeStruct((arranged.shape[0] // 2, quarter), jnp.bfloat16)
    return pl.pallas_call(
        far_kernel,
        out_shape=[half, half],
        scratch_shapes=[pltpu.VMEM((depth, quarter), jnp.bfloat16)],
        compiler_params=params(12),
        cost_estimate=cost(2 * arranged.shape[0] * depth * quarter, 4 << 20),
    )(total, arranged[:, depth:], *blocks)


def body(out_grad, expert_ids, combine, hidden):
    planes = lax.axis_size("dp")
    experts = lax.axis_size("expert")
    out_grad = out_grad.T
    features = out_grad.shape[0]
    hidden = hidden[0]
    share, units = hidden.shape
    capacity = share * planes
    quarter = units // 4
    z = lax.axis_index("dp")
    even = z % 2 == 0

    swap_a = [(i, i ^ 1) for i in range(planes)]
    swap_b = [(i, ((i + 1) ^ 1) - 1) for i in range(planes)]
    swap_b = [(i, j % planes) for i, j in swap_b]
    right = [(i, (i + 2) % planes) for i in range(planes)]
    left = [(i, (i - 2) % planes) for i in range(planes)]

    q = [hidden[:, i * quarter : (i + 1) * quarter] for i in range(4)]
    keep_a, give_a = jnp.where(even, q[0], q[1]), jnp.where(even, q[1], q[0])
    keep_b, give_b = jnp.where(even, q[3], q[2]), jnp.where(even, q[2], q[3])
    got_a = lax.ppermute(give_a, "dp", swap_a)
    got_b = lax.ppermute(give_b, "dp", swap_b)
    grad_a = lax.ppermute(out_grad, "dp", swap_a)
    grad_b = lax.ppermute(out_grad, "dp", swap_b)
    block_a = jnp.concatenate([jnp.where(even, keep_a, got_a), jnp.where(even, got_a, keep_a)])
    block_b = jnp.concatenate([jnp.where(even, got_b, keep_b), jnp.where(even, keep_b, got_b)])

    chain_a, chain_b = {0: block_a}, {0: block_b}
    half = PAIRS // 2
    near = half // 2
    for s in range(1, half + 1):
        chain_a[PAIRS - s] = lax.ppermute(chain_a[(1 - s) % PAIRS], "dp", right)
        if s < half:
            chain_a[s] = lax.ppermute(chain_a[s - 1], "dp", left)
        if s == 2:
            ids = after(after(expert_ids, chain_a, 1), chain_b, 1)
            rows = scaled_rows(out_grad, ids, combine, grad_a, grad_b, experts)
            (rows,) = before([rows], chain_b, 1)
        if s == 3:
            rows = after(after(rows, chain_a, 2), chain_b, 2)
            rows = lax.all_to_all(rows, "expert", split_axis=0, concat_axis=0, tiled=True)
        if s == 6:
            rows = after(rows, chain_b, 5)
            arranged = place(rows, even, z, share, near, features, capacity)
            arranged = before(arranged, chain_b, 5)
        if s == 7:
            total_b = near_product(chain_b, after(arranged[1], chain_b, 6), near)
            (total_b,) = before([total_b], chain_b, 6)
        if s == 8:
            total_a = near_product(chain_a, after(arranged[0], chain_b, 7), near)
            (total_a,) = before([total_a], chain_b, 7)
            totals = total_a, total_b
        if s < half:
            chain_b[PAIRS - s] = lax.ppermute(chain_b[(1 - s) % PAIRS], "dp", right)
        chain_b[s] = lax.ppermute(chain_b[s - 1], "dp", left)

    results = [
        far_product(t, c, a, near) for t, c, a in zip(totals, (chain_a, chain_b), arranged)
    ]
    (theirs_a, mine_a), (mine_b, theirs_b) = results
    back_a = lax.ppermute(theirs_a, "dp", swap_a)
    back_b = lax.ppermute(theirs_b, "dp", swap_b)
    out = jnp.concatenate(
        [
            jnp.where(even, mine_a, back_a),
            jnp.where(even, back_a, mine_a),
            jnp.where(even, back_b, mine_b),
            jnp.where(even, mine_b, back_b),
        ],
        axis=1,
    )
    return out.T[None]


def solution(mesh):
    return jax.shard_map(
        body,
        mesh=mesh,
        in_specs=(
            P("expert", "dp"),
            P("expert", None),
            P("expert", None),
            P("expert", "dp", "tensor"),
        ),
        out_specs=P("expert", "tensor", "dp"),
        check_vma=False,
    )
```

```python
import jax
import jax.numpy as jnp
from jax import lax
from jax.experimental import pallas as pl
from jax.experimental.pallas import tpu as pltpu
from jax.sharding import PartitionSpec as P

TOP = 2


def prefix(array, axis, combine, identity):
    size, place = (lax.axis_size(axis), lax.axis_index(axis))
    everything = lax.all_gather(array, axis)
    start = jnp.broadcast_to(jnp.asarray(identity, array.dtype), array.shape)

    def hop(k, before):
        reached = k < place
        new = combine(before, everything[k])
        return jnp.where(reached, new, before)

    return lax.fori_loop(0, size, hop, start)


def add_counts(earlier, later):
    return earlier + later


def product_kernel(left_ref, right_ref, out_ref):
    out_ref[...] = jnp.dot(
        left_ref[...], right_ref[...], preferred_element_type=jnp.float32
    ).astype(out_ref.dtype)


def product(left, right):
    rows, depth = left.shape
    columns = right.shape[1]
    width = 512
    return pl.pallas_call(
        product_kernel,
        out_shape=jax.ShapeDtypeStruct((rows, columns), jnp.bfloat16),
        grid=(columns // width,),
        in_specs=[
            pl.BlockSpec((rows, depth), lambda i: (0, 0)),
            pl.BlockSpec((depth, width), lambda i: (0, i)),
        ],
        out_specs=pl.BlockSpec((rows, width), lambda i: (0, i)),
        compiler_params=pltpu.CompilerParams(vmem_limit_bytes=16 << 20),
        cost_estimate=pl.CostEstimate(
            flops=2 * rows * depth * columns,
            bytes_accessed=2 * (rows * depth + depth * columns + rows * columns),
            transcendentals=0,
        ),
    )(left, right)


def body(out_grad, expert_ids, combine, hidden):
    experts = lax.axis_size("expert")
    features = out_grad.shape[1]
    capacity = hidden.shape[1] * lax.axis_size("dp")
    block_most = 3 * out_grad.shape[0] * TOP // (2 * experts)
    expert_range = jnp.arange(experts, dtype=jnp.int32)
    gradient, routed, weights = (out_grad, expert_ids, combine)
    onehot = (routed.reshape(-1)[:, None] == expert_range[None, :]).astype(jnp.int32)
    counts = jnp.sum(onehot, axis=0)
    offsets = prefix(counts, "expert", add_counts, jnp.zeros_like(counts))
    local_rank = jnp.sum((jnp.cumsum(onehot, axis=0) - onehot) * onehot, axis=1)
    slot_number = jnp.sum(onehot * offsets[None, :], axis=1) + local_rank
    scaled = (
        (weights[:, :, None] * gradient[:, None, :].astype(jnp.float32))
        .astype(jnp.bfloat16)
        .reshape(-1, features)
    )
    send_index = routed.reshape(-1) * block_most + local_rank
    send_rows = jnp.zeros((experts * block_most, features), jnp.bfloat16).at[send_index].set(scaled)
    send_slots = (
        jnp.full((experts * block_most,), capacity, jnp.int32).at[send_index].set(slot_number)
    )
    send_rows = send_rows.reshape(experts, block_most, features)
    send_slots = send_slots.reshape(experts, block_most)
    arrived_rows, arrived_slots = (
        lax.all_to_all(send_rows, "expert", split_axis=0, concat_axis=0, tiled=True),
        lax.all_to_all(send_slots, "expert", split_axis=0, concat_axis=0, tiled=True),
    )
    arranged = jnp.zeros((capacity + 1, features), jnp.bfloat16)
    arranged = arranged.at[arrived_slots.reshape(-1)].set(arrived_rows.reshape(-1, features))[
        :capacity
    ]
    gathered = lax.all_gather(hidden[0], "dp", axis=0, tiled=True)
    return product(arranged.T, gathered).T[None]


def solution(mesh):
    return jax.shard_map(
        body,
        mesh=mesh,
        in_specs=(
            P("expert", "dp"),
            P("expert", None),
            P("expert", None),
            P("expert", "dp", "tensor"),
        ),
        out_specs=P("expert", "tensor", "dp"),
        check_vma=False,
    )
```

```python
import jax
import jax.numpy as jnp
from jax import lax
from jax.experimental import pallas as pl
from jax.experimental.pallas import tpu as pltpu
from jax.sharding import PartitionSpec as P

LANES = 256
PAIRS = 16
CUT = 1280
COUNT = 192


def dot(a, b, da=1, db=0):
    return lax.dot_general(a, b, (((da,), (db,)), ((), ())), preferred_element_type=jnp.float32)


def send_kernel(ids_ref, weights_ref, own_ref, partner_ref, out_ref):
    features, tokens = own_ref.shape
    experts = out_ref.shape[0]
    ids, weights = ids_ref[...], weights_ref[...]
    lane = lax.broadcasted_iota(jnp.int32, (tokens, 128), 1)
    named = (ids[:, 0:1] == lane) | (ids[:, 1:2] == lane)
    earlier = lax.broadcasted_iota(jnp.int32, (tokens, tokens), 1) < lax.broadcasted_iota(
        jnp.int32, (tokens, tokens), 0
    )
    member = jnp.where(named, 1.0, 0.0).astype(jnp.bfloat16)
    ranks = dot(jnp.where(earlier, 1.0, 0.0).astype(jnp.bfloat16), member).astype(jnp.int32)
    ranks = jnp.where(named, ranks, -1)
    place = lax.broadcasted_iota(jnp.int32, (tokens, LANES), 1)
    for e in range(experts):
        chosen = place == ranks[:, e : e + 1]
        weight = jnp.where(ids[:, 0:1] == e, weights[:, 0:1], weights[:, 1:2])
        scale = jnp.sum(jnp.where(chosen, weight, 0.0), axis=0, keepdims=True)
        count = jnp.sum(jnp.where(ranks[:, e : e + 1] >= 0, 1.0, 0.0), axis=0, keepdims=True)
        pick = jnp.where(chosen, 1.0, 0.0).astype(jnp.bfloat16)
        at_count = lax.broadcasted_iota(jnp.int32, (features, LANES), 1) == COUNT
        for part, ref in enumerate((own_ref, partner_ref)):
            rows = dot(ref[...], pick) * scale
            out_ref[e, part * features : (part + 1) * features, :] = jnp.where(
                at_count, count, rows
            ).astype(jnp.bfloat16)


def place_kernel(base_ref, rows_ref, a_ref, b_ref, sums_a, sums_b):
    sources, wide, _ = rows_ref.shape
    height, capacity = a_ref.shape
    span = sums_a.shape[1] - capacity
    low = wide - height
    sums_a[...] = jnp.zeros_like(sums_a)
    sums_b[...] = jnp.zeros_like(sums_b)
    rank = lax.broadcasted_iota(jnp.int32, (LANES, 1), 0)
    lane = lax.broadcasted_iota(jnp.int32, (LANES, span), 1)
    spare = lax.broadcasted_iota(jnp.int32, (16, 128), 1) == COUNT - 128

    def source(i, offset):
        counts = rows_ref[i, 0:16, 128:256].astype(jnp.float32)
        count = jnp.max(jnp.where(spare, counts, 0.0)).astype(jnp.int32)
        for base, sums, rows in (
            (base_ref[0], sums_a, rows_ref[i, 0:height, :]),
            (base_ref[1], sums_b, rows_ref[i, low:, :]),
        ):
            slot = offset - base
            slot = jnp.where(slot < 0, slot + capacity, slot)
            start = pl.multiple_of((slot // 128) * 128, 128)
            goal = jnp.where(rank < count, rank + (slot - start), -1)
            pick = jnp.where(goal == lane, 1.0, 0.0).astype(jnp.bfloat16)
            sums[:, pl.ds(start, span)] += dot(rows, pick)
        return offset + count

    lax.fori_loop(0, sources, source, jnp.int32(0))
    for sums, out in ((sums_a, a_ref), (sums_b, b_ref)):
        out[:, 0:span] = (sums[:, 0:span] + sums[:, capacity:]).astype(jnp.bfloat16)
        out[:, span:] = sums[:, span:capacity].astype(jnp.bfloat16)


def near_kernel(*refs):
    arranged, blocks, out, held = refs[0], refs[1:-2], refs[-2], refs[-1]
    size = blocks[0].shape[0]
    for i, block in enumerate(blocks):
        held[i * size : (i + 1) * size, :] = block[...]
    out[...] = dot(arranged[...], held[...])


def far_kernel(*refs):
    total, arranged, blocks, (top, bottom), held = refs[0], refs[1], refs[2:-3], refs[-3:-1], refs[-1]
    size = blocks[0].shape[0]
    for i, block in enumerate(blocks):
        held[i * size : (i + 1) * size, :] = block[...]
    half = top.shape[0]
    top[...] = (total[0:half, :] + dot(arranged[0:half, :], held[...])).astype(jnp.bfloat16)
    bottom[...] = (total[half:, :] + dot(arranged[half:, :], held[...])).astype(jnp.bfloat16)


def params(megabytes):
    return pltpu.CompilerParams(vmem_limit_bytes=megabytes << 20)


def cost(flops, bytes_accessed):
    return pl.CostEstimate(flops=flops, bytes_accessed=bytes_accessed, transcendentals=0)


def scaled_rows(own, expert_ids, combine, partner, experts):
    features, tokens = own.shape
    wide = 2 * features
    return pl.pallas_call(
        send_kernel,
        out_shape=jax.ShapeDtypeStruct((experts, wide, LANES), jnp.bfloat16),
        compiler_params=params(12),
        cost_estimate=cost(2 * experts * LANES * tokens * wide, 6 << 20),
    )(expert_ids, combine, own, partner)


def place(rows, bases, capacity):
    experts, wide, _ = rows.shape
    table = jax.ShapeDtypeStruct((wide, capacity), jnp.bfloat16)
    return pl.pallas_call(
        place_kernel,
        out_shape=[table, table],
        in_specs=[
            pl.BlockSpec(memory_space=pltpu.SMEM),
            pl.BlockSpec(memory_space=pltpu.VMEM),
        ],
        scratch_shapes=[pltpu.VMEM((wide, capacity + 384), jnp.float32)] * 2,
        compiler_params=params(16),
        cost_estimate=cost(4 * wide * experts * LANES * 384, 6 << 20),
    )(bases, rows)


def after(value, chain, s):
    return lax.optimization_barrier((value, chain[s], chain[PAIRS - s]))[0]


def before(values, chain, s):
    *values, chain[s], chain[PAIRS - s] = lax.optimization_barrier(
        (*values, chain[s], chain[PAIRS - s])
    )
    return values


def near_product(chain, arranged, near):
    depth = arranged.shape[1] // 2
    blocks = [chain[(d - near) % PAIRS] for d in range(2 * near)]
    quarter = blocks[0].shape[1]
    return pl.pallas_call(
        near_kernel,
        out_shape=jax.ShapeDtypeStruct((arranged.shape[0], quarter), jnp.float32),
        scratch_shapes=[pltpu.VMEM((depth, quarter), jnp.bfloat16)],
        compiler_params=params(12),
        cost_estimate=cost(2 * arranged.shape[0] * depth * quarter, 4 << 20),
    )(arranged[:, :depth], *blocks)


def far_product(total, chain, arranged, near):
    depth = arranged.shape[1] // 2
    blocks = [chain[(d - near) % PAIRS] for d in range(2 * near, PAIRS)]
    quarter = blocks[0].shape[1]
    half = jax.ShapeDtypeStruct((arranged.shape[0] // 2, quarter), jnp.bfloat16)
    return pl.pallas_call(
        far_kernel,
        out_shape=[half, half],
        scratch_shapes=[pltpu.VMEM((depth, quarter), jnp.bfloat16)],
        compiler_params=params(12),
        cost_estimate=cost(2 * arranged.shape[0] * depth * quarter, 4 << 20),
    )(total, arranged[:, depth:], *blocks)


def body(out_grad, expert_ids, combine, hidden):
    planes = lax.axis_size("dp")
    experts = lax.axis_size("expert")
    out_grad = out_grad.T
    features = out_grad.shape[0]
    hidden = hidden[0]
    share, units = hidden.shape
    capacity = share * planes
    half = units // 2
    z = lax.axis_index("dp")
    even = z % 2 == 0

    swap = [(i, i ^ 1) for i in range(planes)]
    right = [(i, (i + 2) % planes) for i in range(planes)]
    left = [(i, (i - 2) % planes) for i in range(planes)]
    keep = jnp.where(even, hidden[:, :half], hidden[:, half:])
    give = jnp.where(even, hidden[:, half:], hidden[:, :half])

    got = lax.ppermute(give, "dp", swap)
    block = jnp.concatenate([jnp.where(even, keep, got), jnp.where(even, got, keep)])

    parity = [list(range(r, planes, 2)) for r in range(2)]
    gathered = lax.all_gather(
        block[:, :CUT], "dp", axis=0, tiled=True, axis_index_groups=parity
    )

    chain = {0: block[:, CUT:]}
    steps = PAIRS // 2
    near = steps // 2
    for s in range(1, steps + 1):
        if s == 2:
            out_grad = after(out_grad, chain, 1)
            partner = lax.ppermute(out_grad, "dp", swap)
        if s == 3:
            ids = after(expert_ids, chain, 2)
            rows = scaled_rows(out_grad, ids, combine, partner, experts)
        if s == 4:
            rows = after(rows, chain, 3)
            rows = lax.all_to_all(rows, "expert", split_axis=0, concat_axis=0, tiled=True)
        if s == 6:
            base = share * (jnp.where(even, z, z - 1) - 2 * near)
            bases = jnp.stack([jnp.int32(0), base % capacity]).astype(jnp.int32)
            plain, turned = place(after(rows, chain, 5), bases, capacity)
            plain, turned = before([plain, turned], chain, 5)
        if s == 7:
            total = near_product(chain, after(turned, chain, 6), near)
            (total,) = before([total], chain, 6)
        chain[PAIRS - s] = lax.ppermute(chain[(1 - s) % PAIRS], "dp", right)
        if s < steps:
            chain[s] = lax.ppermute(chain[s - 1], "dp", left)
    mine_last, theirs_last = far_product(total, chain, turned, near)
    back_last = lax.ppermute(theirs_last, "dp", swap)

    gathered = lax.optimization_barrier((gathered, chain[steps]))[0]
    first = dot(plain, gathered).astype(jnp.bfloat16)
    back_first = lax.ppermute(first[features:], "dp", swap)
    mine = jnp.concatenate([first[:features], mine_last], axis=1)
    back = jnp.concatenate([back_first, back_last], axis=1)
    out = jnp.concatenate([jnp.where(even, mine, back), jnp.where(even, back, mine)], axis=1)
    return out.T[None]


def solution(mesh):
    return jax.shard_map(
        body,
        mesh=mesh,
        in_specs=(
            P("expert", "dp"),
            P("expert", None),
            P("expert", None),
            P("expert", "dp", "tensor"),
        ),
        out_specs=P("expert", "tensor", "dp"),
        check_vma=False,
    )
```

```python
import jax
import jax.numpy as jnp
from jax import lax
from jax.experimental import pallas as pl
from jax.experimental.pallas import tpu as pltpu
from jax.sharding import PartitionSpec as P

TOP = 2


def prefix(array, axis, combine, identity):
    size, place = (lax.axis_size(axis), lax.axis_index(axis))
    everything = lax.all_gather(array, axis)
    start = jnp.broadcast_to(jnp.asarray(identity, array.dtype), array.shape)

    def hop(k, before):
        reached = k < place
        new = combine(before, everything[k])
        return jnp.where(reached, new, before)

    return lax.fori_loop(0, size, hop, start)


def add_counts(earlier, later):
    return earlier + later


def product_kernel(left_ref, right_ref, out_ref, held, arrived):
    blocks = arrived.shape[0]
    width = held.shape[1] // blocks
    spans = [slice(i * width, (i + 1) * width) for i in range(blocks)]
    copies = [
        pltpu.make_async_copy(right_ref.at[:, span], held.at[:, span], arrived.at[i])
        for i, span in enumerate(spans)
    ]
    for copy in copies:
        copy.start()
    for copy, span in zip(copies, spans):
        copy.wait()
        out_ref[:, span] = jnp.dot(
            left_ref[...], held[:, span], preferred_element_type=jnp.float32
        ).astype(out_ref.dtype)


def product(left, right):
    rows, depth = left.shape
    columns = right.shape[1]
    return pl.pallas_call(
        product_kernel,
        out_shape=jax.ShapeDtypeStruct((rows, columns), jnp.bfloat16),
        in_specs=[
            pl.BlockSpec(memory_space=pltpu.VMEM),
            pl.BlockSpec(memory_space=pl.ANY),
        ],
        out_specs=pl.BlockSpec(memory_space=pltpu.VMEM),
        scratch_shapes=[
            pltpu.VMEM((depth, columns), jnp.bfloat16),
            pltpu.SemaphoreType.DMA((8,)),
        ],
        compiler_params=pltpu.CompilerParams(vmem_limit_bytes=56 << 20),
        cost_estimate=pl.CostEstimate(
            flops=2 * rows * depth * columns,
            bytes_accessed=2 * (rows * depth + depth * columns + rows * columns),
            transcendentals=0,
        ),
    )(left, right)


def body(out_grad, expert_ids, combine, hidden):
    experts = lax.axis_size("expert")
    features = out_grad.shape[1]
    capacity = hidden.shape[1] * lax.axis_size("dp")
    block_most = 3 * out_grad.shape[0] * TOP // (2 * experts)
    expert_range = jnp.arange(experts, dtype=jnp.int32)
    gradient, routed, weights = (out_grad, expert_ids, combine)
    onehot = (routed.reshape(-1)[:, None] == expert_range[None, :]).astype(jnp.int32)
    counts = jnp.sum(onehot, axis=0)
    offsets = prefix(counts, "expert", add_counts, jnp.zeros_like(counts))
    local_rank = jnp.sum((jnp.cumsum(onehot, axis=0) - onehot) * onehot, axis=1)
    slot_number = jnp.sum(onehot * offsets[None, :], axis=1) + local_rank
    scaled = (
        (weights[:, :, None] * gradient[:, None, :].astype(jnp.float32))
        .astype(jnp.bfloat16)
        .reshape(-1, features)
    )
    send_index = routed.reshape(-1) * block_most + local_rank
    send_rows = jnp.zeros((experts * block_most, features), jnp.bfloat16).at[send_index].set(scaled)
    send_slots = (
        jnp.full((experts * block_most,), capacity, jnp.int32).at[send_index].set(slot_number)
    )
    send_rows = send_rows.reshape(experts, block_most, features)
    send_slots = send_slots.reshape(experts, block_most)
    arrived_rows, arrived_slots = (
        lax.all_to_all(send_rows, "expert", split_axis=0, concat_axis=0, tiled=True),
        lax.all_to_all(send_slots, "expert", split_axis=0, concat_axis=0, tiled=True),
    )
    arranged = jnp.zeros((capacity + 1, features), jnp.bfloat16)
    arranged = arranged.at[arrived_slots.reshape(-1)].set(arrived_rows.reshape(-1, features))[
        :capacity
    ]
    gathered = lax.all_gather(hidden[0], "dp", axis=0, tiled=True)
    return product(arranged.T, gathered).T[None]


def solution(mesh):
    return jax.shard_map(
        body,
        mesh=mesh,
        in_specs=(
            P("expert", "dp"),
            P("expert", None),
            P("expert", None),
            P("expert", "dp", "tensor"),
        ),
        out_specs=P("expert", "tensor", "dp"),
        check_vma=False,
    )
```

```python
import jax
import jax.numpy as jnp
from jax import lax
from jax.experimental import pallas as pl
from jax.experimental.pallas import tpu as pltpu
from jax.sharding import PartitionSpec as P

TOP = 2
SMALL = (256, 256)


def prefix(array, axis, combine, identity):
    size, place = (lax.axis_size(axis), lax.axis_index(axis))
    everything = lax.all_gather(array, axis)
    start = jnp.broadcast_to(jnp.asarray(identity, array.dtype), array.shape)

    def hop(k, before):
        reached = k < place
        new = combine(before, everything[k])
        return jnp.where(reached, new, before)

    return lax.fori_loop(0, size, hop, start)


def add_counts(earlier, later):
    return earlier + later


def product_kernel(left_ref, right_ref, *refs):
    *parts, out_ref, held, arrived = refs
    blocks = arrived.shape[0]
    width = held.shape[1] // blocks
    spans = [slice(i * width, (i + 1) * width) for i in range(blocks)]
    copies = [
        pltpu.make_async_copy(right_ref.at[:, span], held.at[:, span], arrived.at[i])
        for i, span in enumerate(spans)
    ]
    for copy in copies:
        copy.start()
    start = held.shape[1]
    for part in parts:
        out_ref[:, start : start + part.shape[1]] = part[...]
        start += part.shape[1]
    for copy, span in zip(copies, spans):
        copy.wait()
        out_ref[:, span] = jnp.dot(
            left_ref[...], held[:, span], preferred_element_type=jnp.float32
        ).astype(out_ref.dtype)


def product(left, right, parts):
    rows, depth = left.shape
    columns = right.shape[1]
    width = columns + sum(part.shape[1] for part in parts)
    return pl.pallas_call(
        product_kernel,
        out_shape=jax.ShapeDtypeStruct((rows, width), jnp.bfloat16),
        in_specs=[
            pl.BlockSpec(memory_space=pltpu.VMEM),
            pl.BlockSpec(memory_space=pl.ANY),
            *[pl.BlockSpec(memory_space=pltpu.VMEM)] * len(parts),
        ],
        out_specs=pl.BlockSpec(memory_space=pltpu.VMEM),
        scratch_shapes=[
            pltpu.VMEM((depth, columns), jnp.bfloat16),
            pltpu.SemaphoreType.DMA((columns // 512,)),
        ],
        compiler_params=pltpu.CompilerParams(vmem_limit_bytes=56 << 20),
        cost_estimate=pl.CostEstimate(
            flops=2 * rows * depth * columns,
            bytes_accessed=2 * (rows * depth + depth * columns + rows * columns),
            transcendentals=0,
        ),
    )(left, right, *parts)


def body(out_grad, expert_ids, combine, hidden):
    experts = lax.axis_size("expert")
    features = out_grad.shape[1]
    capacity = hidden.shape[1] * lax.axis_size("dp")
    block_most = 3 * out_grad.shape[0] * TOP // (2 * experts)
    expert_range = jnp.arange(experts, dtype=jnp.int32)
    gradient, routed, weights = (out_grad, expert_ids, combine)
    onehot = (routed.reshape(-1)[:, None] == expert_range[None, :]).astype(jnp.int32)
    counts = jnp.sum(onehot, axis=0)
    offsets = prefix(counts, "expert", add_counts, jnp.zeros_like(counts))
    local_rank = jnp.sum((jnp.cumsum(onehot, axis=0) - onehot) * onehot, axis=1)
    slot_number = jnp.sum(onehot * offsets[None, :], axis=1) + local_rank
    scaled = (
        (weights[:, :, None] * gradient[:, None, :].astype(jnp.float32))
        .astype(jnp.bfloat16)
        .reshape(-1, features)
    )
    send_index = routed.reshape(-1) * block_most + local_rank
    send_rows = jnp.zeros((experts * block_most, features), jnp.bfloat16).at[send_index].set(scaled)
    send_slots = (
        jnp.full((experts * block_most,), capacity, jnp.int32).at[send_index].set(slot_number)
    )
    send_rows = send_rows.reshape(experts, block_most, features)
    send_slots = send_slots.reshape(experts, block_most)
    arrived_rows, arrived_slots = (
        lax.all_to_all(send_rows, "expert", split_axis=0, concat_axis=0, tiled=True),
        lax.all_to_all(send_slots, "expert", split_axis=0, concat_axis=0, tiled=True),
    )
    arranged = jnp.zeros((capacity + 1, features), jnp.bfloat16)
    arranged = arranged.at[arrived_slots.reshape(-1)].set(arrived_rows.reshape(-1, features))[
        :capacity
    ]
    hidden = hidden[0]
    most = hidden.shape[1] - sum(SMALL)
    gathered = lax.all_gather(hidden[:, :most], "dp", axis=0, tiled=True)
    parts, start = [], most
    for width in SMALL:
        some = lax.all_gather(hidden[:, start : start + width], "dp", axis=0, tiled=True)
        parts.append(dot(arranged, some))
        start += width
    return product(arranged.T, gathered, parts).T[None]


def dot(left, right):
    return lax.dot_general(
        left, right, (((0,), (0,)), ((), ())), preferred_element_type=jnp.float32
    ).astype(jnp.bfloat16)


def solution(mesh):
    return jax.shard_map(
        body,
        mesh=mesh,
        in_specs=(
            P("expert", "dp"),
            P("expert", None),
            P("expert", None),
            P("expert", "dp", "tensor"),
        ),
        out_specs=P("expert", "tensor", "dp"),
        check_vma=False,
    )
```

```python
import jax
import jax.numpy as jnp
from jax import lax
from jax.experimental import pallas as pl
from jax.experimental.pallas import tpu as pltpu
from jax.sharding import PartitionSpec as P

TOP = 2
SMALL = (256,)


def prefix(array, axis, combine, identity):
    size, place = (lax.axis_size(axis), lax.axis_index(axis))
    everything = lax.all_gather(array, axis)
    start = jnp.broadcast_to(jnp.asarray(identity, array.dtype), array.shape)

    def hop(k, before):
        reached = k < place
        new = combine(before, everything[k])
        return jnp.where(reached, new, before)

    return lax.fori_loop(0, size, hop, start)


def add_counts(earlier, later):
    return earlier + later


def product_kernel(left_ref, right_ref, *refs):
    *parts, out_ref, held, arrived = refs
    blocks = arrived.shape[0]
    width = held.shape[1] // blocks
    spans = [slice(i * width, (i + 1) * width) for i in range(blocks)]
    copies = [
        pltpu.make_async_copy(right_ref.at[:, span], held.at[:, span], arrived.at[i])
        for i, span in enumerate(spans)
    ]
    for copy in copies:
        copy.start()
    start = held.shape[1]
    for part in parts:
        out_ref[:, start : start + part.shape[1]] = part[...]
        start += part.shape[1]
    for copy, span in zip(copies, spans):
        copy.wait()
        out_ref[:, span] = jnp.dot(
            left_ref[...], held[:, span], preferred_element_type=jnp.float32
        ).astype(out_ref.dtype)


def product(left, right, parts):
    rows, depth = left.shape
    columns = right.shape[1]
    width = columns + sum(part.shape[1] for part in parts)
    return pl.pallas_call(
        product_kernel,
        out_shape=jax.ShapeDtypeStruct((rows, width), jnp.bfloat16),
        in_specs=[
            pl.BlockSpec(memory_space=pltpu.VMEM),
            pl.BlockSpec(memory_space=pl.ANY),
            *[pl.BlockSpec(memory_space=pltpu.VMEM)] * len(parts),
        ],
        out_specs=pl.BlockSpec(memory_space=pltpu.VMEM),
        scratch_shapes=[
            pltpu.VMEM((depth, columns), jnp.bfloat16),
            pltpu.SemaphoreType.DMA((columns // 640,)),
        ],
        compiler_params=pltpu.CompilerParams(vmem_limit_bytes=56 << 20),
        cost_estimate=pl.CostEstimate(
            flops=2 * rows * depth * columns,
            bytes_accessed=2 * (rows * depth + depth * columns + rows * columns),
            transcendentals=0,
        ),
    )(left, right, *parts)


def body(out_grad, expert_ids, combine, hidden):
    experts = lax.axis_size("expert")
    features = out_grad.shape[1]
    capacity = hidden.shape[1] * lax.axis_size("dp")
    block_most = 3 * out_grad.shape[0] * TOP // (2 * experts)
    expert_range = jnp.arange(experts, dtype=jnp.int32)
    gradient, routed, weights = (out_grad, expert_ids, combine)
    onehot = (routed.reshape(-1)[:, None] == expert_range[None, :]).astype(jnp.int32)
    counts = jnp.sum(onehot, axis=0)
    offsets = prefix(counts, "expert", add_counts, jnp.zeros_like(counts))
    local_rank = jnp.sum((jnp.cumsum(onehot, axis=0) - onehot) * onehot, axis=1)
    slot_number = jnp.sum(onehot * offsets[None, :], axis=1) + local_rank
    scaled = (
        (weights[:, :, None] * gradient[:, None, :].astype(jnp.float32))
        .astype(jnp.bfloat16)
        .reshape(-1, features)
    )
    send_index = routed.reshape(-1) * block_most + local_rank
    send_rows = jnp.zeros((experts * block_most, features), jnp.bfloat16).at[send_index].set(scaled)
    send_slots = (
        jnp.full((experts * block_most,), capacity, jnp.int32).at[send_index].set(slot_number)
    )
    send_rows = send_rows.reshape(experts, block_most, features)
    send_slots = send_slots.reshape(experts, block_most)
    arrived_rows, arrived_slots = (
        lax.all_to_all(send_rows, "expert", split_axis=0, concat_axis=0, tiled=True),
        lax.all_to_all(send_slots, "expert", split_axis=0, concat_axis=0, tiled=True),
    )
    arranged = jnp.zeros((capacity + 1, features), jnp.bfloat16)
    arranged = arranged.at[arrived_slots.reshape(-1)].set(arrived_rows.reshape(-1, features))[
        :capacity
    ]
    hidden = hidden[0]
    most = hidden.shape[1] - sum(SMALL)
    gathered = lax.all_gather(hidden[:, :most], "dp", axis=0, tiled=True)
    parts, start = [], most
    for width in SMALL:
        some = lax.all_gather(hidden[:, start : start + width], "dp", axis=0, tiled=True)
        parts.append(dot(arranged, some))
        start += width
    return product(arranged.T, gathered, parts).T[None]


def dot(left, right):
    return lax.dot_general(
        left, right, (((0,), (0,)), ((), ())), preferred_element_type=jnp.float32
    ).astype(jnp.bfloat16)


def solution(mesh):
    return jax.shard_map(
        body,
        mesh=mesh,
        in_specs=(
            P("expert", "dp"),
            P("expert", None),
            P("expert", None),
            P("expert", "dp", "tensor"),
        ),
        out_specs=P("expert", "tensor", "dp"),
        check_vma=False,
    )
```

```python
import jax
import jax.numpy as jnp
from jax import lax
from jax.experimental import pallas as pl
from jax.experimental.pallas import tpu as pltpu
from jax.sharding import PartitionSpec as P

TOP = 2


def prefix(array, axis, combine, identity):
    size, place = (lax.axis_size(axis), lax.axis_index(axis))
    everything = lax.all_gather(array, axis)
    start = jnp.broadcast_to(jnp.asarray(identity, array.dtype), array.shape)

    def hop(k, before):
        reached = k < place
        new = combine(before, everything[k])
        return jnp.where(reached, new, before)

    return lax.fori_loop(0, size, hop, start)


def add_counts(earlier, later):
    return earlier + later


def product_kernel(left_ref, right_ref, out_ref, held, done, arrived, sent):
    blocks = arrived.shape[0]
    width = held.shape[1] // blocks
    spans = [slice(i * width, (i + 1) * width) for i in range(blocks)]
    copies = [
        pltpu.make_async_copy(right_ref.at[:, span], held.at[:, span], arrived.at[i])
        for i, span in enumerate(spans)
    ]
    results = [
        pltpu.make_async_copy(done.at[:, span], out_ref.at[:, span], sent.at[i])
        for i, span in enumerate(spans)
    ]
    for copy in copies:
        copy.start()
    for copy, result, span in zip(copies, results, spans):
        copy.wait()
        done[:, span] = jnp.dot(
            left_ref[...], held[:, span], preferred_element_type=jnp.float32
        ).astype(done.dtype)
        result.start()
    for result in results:
        result.wait()


def product(left, right):
    rows, depth = left.shape
    columns = right.shape[1]
    return pl.pallas_call(
        product_kernel,
        out_shape=jax.ShapeDtypeStruct((rows, columns), jnp.bfloat16),
        in_specs=[
            pl.BlockSpec(memory_space=pltpu.VMEM),
            pl.BlockSpec(memory_space=pl.ANY),
        ],
        out_specs=pl.BlockSpec(memory_space=pl.ANY),
        scratch_shapes=[
            pltpu.VMEM((depth, columns), jnp.bfloat16),
            pltpu.VMEM((rows, columns), jnp.bfloat16),
            pltpu.SemaphoreType.DMA((4,)),
            pltpu.SemaphoreType.DMA((4,)),
        ],
        compiler_params=pltpu.CompilerParams(vmem_limit_bytes=53 << 20),
        cost_estimate=pl.CostEstimate(
            flops=2 * rows * depth * columns,
            bytes_accessed=2 * (rows * depth + depth * columns + rows * columns),
            transcendentals=0,
        ),
    )(left, right)


def body(out_grad, expert_ids, combine, hidden):
    experts = lax.axis_size("expert")
    features = out_grad.shape[1]
    capacity = hidden.shape[1] * lax.axis_size("dp")
    block_most = 3 * out_grad.shape[0] * TOP // (2 * experts)
    expert_range = jnp.arange(experts, dtype=jnp.int32)
    gradient, routed, weights = (out_grad, expert_ids, combine)
    onehot = (routed.reshape(-1)[:, None] == expert_range[None, :]).astype(jnp.int32)
    counts = jnp.sum(onehot, axis=0)
    offsets = prefix(counts, "expert", add_counts, jnp.zeros_like(counts))
    local_rank = jnp.sum((jnp.cumsum(onehot, axis=0) - onehot) * onehot, axis=1)
    slot_number = jnp.sum(onehot * offsets[None, :], axis=1) + local_rank
    scaled = (
        (weights[:, :, None] * gradient[:, None, :].astype(jnp.float32))
        .astype(jnp.bfloat16)
        .reshape(-1, features)
    )
    send_index = routed.reshape(-1) * block_most + local_rank
    send_rows = jnp.zeros((experts * block_most, features), jnp.bfloat16).at[send_index].set(scaled)
    send_slots = (
        jnp.full((experts * block_most,), capacity, jnp.int32).at[send_index].set(slot_number)
    )
    send_rows = send_rows.reshape(experts, block_most, features)
    send_slots = send_slots.reshape(experts, block_most)
    arrived_rows, arrived_slots = (
        lax.all_to_all(send_rows, "expert", split_axis=0, concat_axis=0, tiled=True),
        lax.all_to_all(send_slots, "expert", split_axis=0, concat_axis=0, tiled=True),
    )
    arranged = jnp.zeros((capacity + 1, features), jnp.bfloat16)
    arranged = arranged.at[arrived_slots.reshape(-1)].set(arrived_rows.reshape(-1, features))[
        :capacity
    ]
    gathered = lax.all_gather(hidden[0], "dp", axis=0, tiled=True)
    return product(arranged.T, gathered).T[None]


def solution(mesh):
    return jax.shard_map(
        body,
        mesh=mesh,
        in_specs=(
            P("expert", "dp"),
            P("expert", None),
            P("expert", None),
            P("expert", "dp", "tensor"),
        ),
        out_specs=P("expert", "tensor", "dp"),
        check_vma=False,
    )
```
